256 devices in a mesh: row: 16 (over z, core), col: 16 (over y, x).
Axes of the slice: x: 4, y: 4, z: 8, core: 2. Of those that a mesh axis runs over, the one named last changes fastest.
Arguments:
- iterate: float32 [32768, 256], P(('row', 'col'))
- past_images: float32 [5, 32768, 256], P(None, ('row', 'col'))
- past_residuals: float32 [5, 32768, 256], P(None, ('row', 'col'))
- features: bfloat16 [32768, 128], P(('row', 'col')), may hold values from -6 to 6
- input_weight: bfloat16 [128, 256], replicated, may hold values from -0.5 to 0.5
- mix_weight: bfloat16 [256, 256], replicated, may hold values from -0.375 to 0.375
- tile_values: bfloat16 [16, 16, 256, 128, 128], P('row', 'col'), may hold values from -0.02734375 to 0.02734375
- tile_rows: int32 [16, 16, 256], P('row', 'col'), may hold values from 0 to 15
- tile_cols: int32 [16, 16, 256], P('row', 'col'), may hold values from 0 to 15
- tile_count: int32 [16, 16], P('row', 'col'), may hold values from 1 to 256, as said below
Outputs:
- next_iterate: float32 [32768, 256], P(('row', 'col'))
- last_residual: float32 [32768, 256], P(('row', 'col'))
The draws below stay inside these ranges and needn't reach their ends.
Inputs may be any that keep to these rules, and one draw needn't show every extreme that they name: `tile_count`: live tile slots of a device; some device has exactly 256.
All inputs are finite; a program needn't handle non-finite values.
Results may differ from the reference program's by a relative error of at most 0.015.
Values may be sent and summed in bfloat16 or wider, within the bound.
A program may use at most 64 MiB of HBM per device.

```python
import jax
import jax.numpy as jnp
from jax import lax

CHANNELS = 256
FEATURES = 128
TILE = 128
MEMORY = 5
ITERS = 3
TILES_ROW = 16
NODES_DEV = 128
NODES = 32768
ROW_TILES = 16
COL_TILES = 16
TILES = 256
N_ROW = 16
N_COL = 16


def field_scales(key):
    row_key, col_key = jax.random.split(key)
    ramp = 1.0 + 2.0 * jnp.arange(NODES, dtype=jnp.float32) / NODES
    rows = 10.0 ** (jax.random.uniform(row_key, (NODES,), jnp.float32) - 0.5) * ramp * 0.5
    cols = 10.0 ** (jax.random.uniform(col_key, (CHANNELS,), jnp.float32) - 0.5)
    return rows[:, None] * cols[None, :]


def draw_iterate(key, part):
    key = jax.random.fold_in(key, 11)
    scale_key, base_key = jax.random.split(key)
    base = jax.random.normal(base_key, (NODES, CHANNELS), jnp.float32)
    return base * field_scales(scale_key)


def draw_past_images(key, part):
    key = jax.random.fold_in(key, 23)
    scale_key, base_key = jax.random.split(key, 2)
    base = jax.random.normal(base_key, (MEMORY, NODES, CHANNELS), jnp.float32)
    return jnp.abs(base) * field_scales(scale_key)[None]


def draw_past_residuals(key, part):
    key = jax.random.fold_in(key, 37)
    scale_key, base_key = jax.random.split(key, 2)
    base = jax.random.normal(base_key, (MEMORY, NODES, CHANNELS), jnp.float32)
    return base * field_scales(scale_key)[None]


def draw_tile_count(key, part):
    key = jax.random.fold_in(key, 5)
    count_key, heavy_key = jax.random.split(key)
    counts = jax.random.randint(count_key, (N_ROW * N_COL,), 1, 2 * TILES // 3 + 1, jnp.int32)
    heavy = jax.random.randint(heavy_key, (), 0, N_ROW * N_COL, jnp.int32)
    counts = jnp.where(jnp.arange(N_ROW * N_COL, dtype=jnp.int32) == heavy, TILES, counts)
    return counts.reshape(N_ROW, N_COL).astype(jnp.int32)


def place_ends(entries, rng, least, high):
    extent = entries.shape
    spot = [jax.random.randint(jax.random.fold_in(rng, axis), (), 0, extent[axis]) for axis in range(len(extent))]
    entries = entries.at[tuple(spot)].set(least)
    longest = extent.index(max(extent))
    spot[longest] = (spot[longest] + 1) % extent[longest]
    return entries.at[tuple(spot)].set(high)


def block_levels(own_key, extent, pieces, smallest, top_value):
    gain = 1.0
    for dim, parts in pieces:
        steps = jax.random.uniform(jax.random.fold_in(jax.random.fold_in(own_key, 6), dim), (parts,), jnp.float32, smallest / len(pieces), top_value / len(pieces))
        gain = gain * jnp.repeat(jnp.exp(steps), extent[dim] // parts).reshape((-1,) + (1,) * (len(extent) - 1 - dim))
    return gain


def noise(own_key, dims, deviation, reach, shards=(), kind=jnp.bfloat16):
    array = deviation * jax.random.normal(own_key, dims, jnp.float32)
    if shards:
        array = array * block_levels(own_key, dims, shards, -0.22, 0.18)
    return jnp.clip(array, -reach, reach).astype(kind)


def setup_inputs(seed: int = 0) -> dict:
    key_of = jax.random.split(jax.random.key(seed), 11)
    iterate = draw_iterate(jax.random.fold_in(key_of[10], 71), 0)
    past_images = draw_past_images(jax.random.fold_in(key_of[10], 71), 0)
    past_residuals = draw_past_residuals(jax.random.fold_in(key_of[10], 71), 0)
    features = noise(key_of[3], (NODES, FEATURES), 1.0, 6.0, ((0, 256),))
    input_weight = noise(key_of[4], (FEATURES, CHANNELS), FEATURES ** -0.5, 0.5)
    mix_weight = noise(key_of[5], (CHANNELS, CHANNELS), CHANNELS ** -0.5, 0.375)
    tile_values = noise(key_of[6], (N_ROW, N_COL, TILES, TILE, TILE), (4 * TILES_ROW * N_COL * TILE // 3) ** -0.5, 0.02734375, ((0, 16), (1, 16)))
    tile_rows = place_ends(jax.random.randint(key_of[7], (N_ROW, N_COL, TILES), 0, ROW_TILES), jax.random.fold_in(key_of[7], 1), 0, ROW_TILES - 1).astype(jnp.int32)
    tile_cols = place_ends(jax.random.randint(key_of[8], (N_ROW, N_COL, TILES), 0, COL_TILES), jax.random.fold_in(key_of[8], 1), 0, COL_TILES - 1).astype(jnp.int32)
    tile_count = draw_tile_count(jax.random.fold_in(key_of[10], 71), 0)
    return {"iterate": iterate, "past_images": past_images, "past_residuals": past_residuals, "features": features, "input_weight": input_weight, "mix_weight": mix_weight, "tile_values": tile_values, "tile_rows": tile_rows, "tile_cols": tile_cols, "tile_count": tile_count}


def solve_small(matrix, rhs):
    count = matrix.shape[0]
    lower = {}
    for first in range(count):
        for second in range(first + 1):
            total = matrix[first, second]
            for inner in range(second):
                total = total - lower[first, inner] * lower[second, inner]
            if first == second:
                lower[first, second] = jnp.sqrt(total)
            else:
                lower[first, second] = total / lower[second, second]
    forward = []
    for first in range(count):
        total = rhs[first]
        for inner in range(first):
            total = total - lower[first, inner] * forward[inner]
        forward.append(total / lower[first, first])
    backward = [None] * count
    for first in reversed(range(count)):
        total = forward[first]
        for inner in range(first + 1, count):
            total = total - lower[inner, first] * backward[inner]
        backward[first] = total / lower[first, first]
    return jnp.stack(backward)

def mixing(gram):
    size = gram.shape[0]
    regular = gram + 0.05 * (jnp.trace(gram) / size) * jnp.eye(size, dtype=gram.dtype)
    weights = solve_small(regular, jnp.ones((size,), gram.dtype))
    return weights / jnp.sum(weights)

def aggregate_rows(message, tile_values, tile_rows, tile_cols, tile_count):
    blocks = message.reshape(N_ROW, N_COL, NODES_DEV, CHANNELS)

    def one_row(row_pos):

        def one_device(total, col_pos):
            panel = jnp.take(blocks, col_pos, axis=1).reshape(COL_TILES, TILE, CHANNELS)
            values = tile_values[row_pos, col_pos]
            chosen = panel[tile_cols[row_pos, col_pos]]
            products = jnp.einsum('stu,suh->sth', values.astype(jnp.float32), chosen.astype(jnp.float32))
            live = jnp.arange(TILES, dtype=jnp.int32) < tile_count[row_pos, col_pos]
            products = jnp.where(live[:, None, None], products, jnp.zeros_like(products))
            summed = jax.ops.segment_sum(products, tile_rows[row_pos, col_pos], num_segments=ROW_TILES)
            rounded = summed.reshape(ROW_TILES * TILE, CHANNELS).astype(jnp.bfloat16)
            rounded = lax.optimization_barrier(rounded)
            return (total + rounded.astype(jnp.float32), None)
        start = jnp.zeros((ROW_TILES * TILE, CHANNELS), jnp.float32)
        total, unused = lax.scan(one_device, start, jnp.arange(N_COL, dtype=jnp.int32))
        return total
    rows = lax.map(one_row, jnp.arange(N_ROW, dtype=jnp.int32))
    return rows.reshape(NODES, CHANNELS)

def reference(iterate, past_images, past_residuals, features, input_weight, mix_weight, tile_values, tile_rows, tile_cols, tile_count):
    inject = jnp.dot(features, input_weight, preferred_element_type=jnp.float32)
    state = iterate
    images = past_images
    residuals = past_residuals
    residual = iterate
    for step in range(ITERS):
        lowered = state.astype(jnp.bfloat16)
        message = jnp.dot(lowered, mix_weight, preferred_element_type=jnp.float32).astype(jnp.bfloat16)
        aggregate = aggregate_rows(message, tile_values, tile_rows, tile_cols, tile_count)
        image = jax.nn.relu(aggregate + inject)
        residual = image - state
        images = jnp.concatenate([images[1:], image[None]], axis=0)
        residuals = jnp.concatenate([residuals[1:], residual[None]], axis=0)
        gram = jnp.einsum('anh,bnh->ab', residuals, residuals, precision=lax.Precision.HIGHEST)
        alpha = mixing(gram)
        state = lax.optimization_barrier(jnp.sum(alpha[:, None, None] * images, axis=0))
    return (state, residual)
```

```python
import jax
import jax.numpy as jnp
from jax import lax
from jax.experimental import pallas as pl
from jax.experimental.pallas import tpu as pltpu
from jax.sharding import PartitionSpec as P

ITERS = 3
TILE = 128
HALF = 64
CHANNELS = 256
MESH = pl.DeviceIdType.MESH
F32 = jnp.float32
BF16 = jnp.bfloat16
CHUNKS = 8
SLOTS = 256


def build_kernel(rows_ref, cols_ref, count_ref, values_ref, dense_ref, buf, acc, out, in_sem, out_sem):
    size = SLOTS // CHUNKS
    loads = []
    for chunk in range(CHUNKS):
        span = pl.ds(chunk * size, size)
        loads.append(pltpu.make_async_copy(values_ref.at[span], buf.at[span], in_sem.at[chunk]))
        loads[-1].start()
    count = count_ref[0]

    @pl.loop(0, 256)
    def _(cell):
        acc[cell] = jnp.zeros((TILE, TILE), F32)

    for chunk in range(CHUNKS):
        loads[chunk].wait()

        @pl.loop(chunk * size, jnp.minimum(count, (chunk + 1) * size))
        def _(slot):
            cell = cols_ref[slot] * 16 + rows_ref[slot]
            acc[cell] += buf[slot].astype(F32)

    stores = []
    for col_tile in range(16):

        @pl.loop(0, 16)
        def _(row_tile):
            out[col_tile, row_tile] = acc[col_tile * 16 + row_tile].astype(BF16)

        stores.append(pltpu.make_async_copy(out.at[col_tile], dense_ref.at[col_tile], out_sem.at[col_tile]))
        stores[-1].start()
    for store in stores:
        store.wait()


def build_dense(rows, cols, count, values):
    return pl.pallas_call(
        build_kernel,
        out_shape=jax.ShapeDtypeStruct((16, 16, TILE, TILE), BF16),
        in_specs=[pl.BlockSpec(memory_space=pltpu.SMEM)] * 3 + [pl.BlockSpec(memory_space=pl.ANY)],
        out_specs=pl.BlockSpec(memory_space=pl.ANY),
        scratch_shapes=[
            pltpu.VMEM((SLOTS, TILE, TILE), BF16),
            pltpu.VMEM((256, TILE, TILE), F32),
            pltpu.VMEM((16, 16, TILE, TILE), BF16),
            pltpu.SemaphoreType.DMA((CHUNKS,)),
            pltpu.SemaphoreType.DMA((16,)),
        ],
        compiler_params=pltpu.CompilerParams(vmem_limit_bytes=44 * 1024 * 1024),
        name="build_dense",
    )(rows, cols, count, values)


def mixing_weights(gram):
    trace = gram[0, 0]
    for pos in range(1, 5):
        trace = trace + gram[pos, pos]
    shift = 0.05 * (trace / 5.0)
    lower = {}
    for first in range(5):
        for second in range(first + 1):
            total = gram[first, second]
            if first == second:
                total = total + shift
            for inner in range(second):
                total = total - lower[first, inner] * lower[second, inner]
            if first == second:
                lower[first, second] = jnp.sqrt(total)
            else:
                lower[first, second] = total / lower[second, second]
    forward = []
    for first in range(5):
        total = jnp.ones_like(trace)
        for inner in range(first):
            total = total - lower[first, inner] * forward[inner]
        forward.append(total / lower[first, first])
    backward = [None] * 5
    for first in reversed(range(5)):
        total = forward[first]
        for inner in range(first + 1, 5):
            total = total - lower[inner, first] * backward[inner]
        backward[first] = total / lower[first, first]
    norm = backward[0]
    for pos in range(1, 5):
        norm = norm + backward[pos]
    return [value / norm for value in backward]


OLD_PAIRS = [(first, second) for first in range(4) for second in range(first + 1)]


def lane_sums(left, right):
    return jnp.sum(left[:, :TILE] * right[:, :TILE] + left[:, TILE:] * right[:, TILE:], axis=0, keepdims=True)


def main_kernel(
    iterate_ref, features_ref, input_weight_ref, mix_weight_ref, past_images_ref, past_residuals_ref, dense_ref,
    state_out, residual_out,
    dense, panel, acc, part_a, part_b, got_a1, got_b1, sum_a, sum_b, got_a2, got_b2,
    state, inject, images, residuals, pack, gram_send1, gram_send2, gram_got1, gram_got2,
    load_sem, ag_send, ag_recv, a1_send, a1_recv, b1_send, b1_recv, a2_send, a2_recv, b2_send, b2_recv,
    g1_send, g1_recv, g2_send, g2_recv,
):
    row = lax.axis_index("row")
    col = lax.axis_index("col")
    z, core = row // 2, lax.rem(row, 2)
    y, x = col // 4, lax.rem(col, 4)
    sibling = row + 1 - 2 * core

    load_dense = pltpu.make_async_copy(dense_ref, dense, load_sem.at[0])
    load_images = pltpu.make_async_copy(past_images_ref.at[pl.ds(1, 4)], images.at[pl.ds(0, 4)], load_sem.at[1])
    load_residuals = pltpu.make_async_copy(
        past_residuals_ref.at[pl.ds(1, 4)], residuals.at[pl.ds(0, 4)], load_sem.at[2]
    )
    load_dense.start()
    load_images.start()
    load_residuals.start()

    barrier = pltpu.get_barrier_semaphore()

    @pl.loop(1, 16)
    def _(step):
        pl.semaphore_signal(barrier, inc=1, device_id=(row, lax.rem(col + step, 16)), device_id_type=MESH)
        pl.semaphore_signal(barrier, inc=1, device_id=(lax.rem(row + step, 16), col), device_id_type=MESH)

    state[...] = iterate_ref[...]
    inject[...] = jnp.dot(features_ref[...], input_weight_ref[...], preferred_element_type=F32)
    pack[...] = jnp.zeros_like(pack)
    pl.semaphore_wait(barrier, 30)

    def chip(offset):
        return lax.rem(z + offset + 8, 8)

    @pl.loop(0, ITERS)
    def _(k):
        panel[row] = jnp.dot(state[...].astype(BF16), mix_weight_ref[...], preferred_element_type=F32).astype(BF16)
        sends = []

        def send(src, dst, sem, target):
            copy = pltpu.make_async_remote_copy(
                src_ref=src,
                dst_ref=dst,
                send_sem=ag_send.at[len(sends)],
                recv_sem=sem,
                device_id=(target, col),
                device_id_type=MESH,
            )
            copy.start()
            sends.append(copy)

        def block(tile):
            return panel.at[tile]

        def arrive(tile, ref=None, sem=None):
            ref = block(tile) if ref is None else ref
            sem = ag_recv.at[tile] if sem is None else sem
            pltpu.make_async_copy(ref, ref, sem).wait()

        up, down = 2 * chip(1) + core, 2 * chip(-1) + core
        send(block(row), block(row), ag_recv.at[row], up)
        send(block(row), block(row), ag_recv.at[row], down)
        send(block(row), block(row), ag_recv.at[row], sibling)

        def multiply(pos, first=False, last=False):
            rhs = panel[pl.ds(2 * pos, 2)].reshape(2 * TILE, CHANNELS)

            @pl.loop(0, 4)
            def _(group):
                rows = pl.ds(4 * group, 4)
                left = dense[2 * pos, rows].reshape(4 * TILE, TILE)
                right = dense[2 * pos + 1, rows].reshape(4 * TILE, TILE)
                product = jnp.dot(jnp.concatenate([left, right], axis=1), rhs, preferred_element_type=F32)
                if first:
                    acc[group] = product
                elif not last:
                    acc[group] += product
                else:
                    total = (acc[group] + product).astype(BF16)
                    for tile in range(4):
                        part_a[tile, group] = total[tile * TILE : tile * TILE + HALF]
                        part_b[group, tile] = total[tile * TILE + HALF : (tile + 1) * TILE]

        @pl.when(k == 0)
        def _():
            load_images.wait()
            load_residuals.wait()

        for pos, (first, second) in enumerate(OLD_PAIRS):
            pack[5 + pos : 6 + pos, :] = lane_sums(residuals[k + first], residuals[k + second])

        @pl.when(k == 0)
        def _():
            load_dense.wait()

        low, high = pl.ds(0, HALF), pl.ds(HALF, HALF)
        far = 2 * chip(4) + core
        for step in range(1, 4):
            for sign in (-1, 1):
                tile = 2 * chip(sign * step) + core
                target = up if sign < 0 else down
                arrive(tile)
                if step < 3:
                    send(block(tile), block(tile), ag_recv.at[tile], target)
                else:
                    part = low if sign < 0 else high
                    sem = ag_recv.at[tile] if sign < 0 else ag_recv.at[16]
                    send(panel.at[tile, part], panel.at[tile, part], sem, target)
                send(block(tile), block(tile), ag_recv.at[tile], sibling)
            if step == 1:
                arrive(sibling)
                multiply(z, first=True)
            else:
                for sign in (-1, 1):
                    arrive(2 * chip(sign * (step - 1)) + 1 - core)
                    multiply(chip(sign * (step - 1)))
        for sign in (-1, 1):
            arrive(2 * chip(sign * 3) + 1 - core)
            multiply(chip(sign * 3))
        arrive(far, panel.at[far, low])
        arrive(far, panel.at[far, high], ag_recv.at[16])
        send(block(far), block(far), ag_recv.at[far], sibling)
        arrive(2 * chip(4) + 1 - core)
        multiply(chip(4), last=True)

        copies = []
        for step in range(1, 4):
            to_x, to_y = lax.rem(x + step, 4), lax.rem(y + step, 4)
            copies.append(pltpu.make_async_remote_copy(
                src_ref=part_a.at[to_x], dst_ref=got_a1.at[x], send_sem=a1_send.at[step], recv_sem=a1_recv.at[x],
                device_id=(row, 4 * y + to_x), device_id_type=MESH,
            ))
            copies.append(pltpu.make_async_remote_copy(
                src_ref=part_b.at[to_y], dst_ref=got_b1.at[y], send_sem=b1_send.at[step], recv_sem=b1_recv.at[y],
                device_id=(row, 4 * to_y + x), device_id_type=MESH,
            ))
        for copy in copies:
            copy.start()
        for copy in sends:
            copy.wait_send()
        for step in range(1, 4):
            from_x, from_y = lax.rem(x + 4 - step, 4), lax.rem(y + 4 - step, 4)
            pltpu.make_async_copy(got_a1.at[from_x], got_a1.at[from_x], a1_recv.at[from_x]).wait()
            pltpu.make_async_copy(got_b1.at[from_y], got_b1.at[from_y], b1_recv.at[from_y]).wait()
        for step in range(1, 5):
            to_x, to_y = lax.rem(x + step, 4), lax.rem(y + step, 4)
            total_a = part_a[x, to_y].astype(F32)
            total_b = part_b[y, to_x].astype(F32)
            for other in range(1, 4):
                total_a += got_a1[lax.rem(x + other, 4), to_y].astype(F32)
                total_b += got_b1[lax.rem(y + other, 4), to_x].astype(F32)
            sum_a[to_y] = total_a.astype(BF16)
            sum_b[to_x] = total_b.astype(BF16)
            if step == 4:
                break
            copy_a = pltpu.make_async_remote_copy(
                src_ref=sum_a.at[to_y], dst_ref=got_a2.at[y], send_sem=a2_send.at[step], recv_sem=a2_recv.at[y],
                device_id=(row, 4 * to_y + x), device_id_type=MESH,
            )
            copy_b = pltpu.make_async_remote_copy(
                src_ref=sum_b.at[to_x], dst_ref=got_b2.at[x], send_sem=b2_send.at[step], recv_sem=b2_recv.at[x],
                device_id=(row, 4 * y + to_x), device_id_type=MESH,
            )
            copy_a.start()
            copy_b.start()
            copies += [copy_a, copy_b]
        for step in range(1, 4):
            from_x, from_y = lax.rem(x + 4 - step, 4), lax.rem(y + 4 - step, 4)
            pltpu.make_async_copy(got_a2.at[from_y], got_a2.at[from_y], a2_recv.at[from_y]).wait()
            pltpu.make_async_copy(got_b2.at[from_x], got_b2.at[from_x], b2_recv.at[from_x]).wait()
        total_a = sum_a[y].astype(F32)
        total_b = sum_b[x].astype(F32)
        for other in range(1, 4):
            total_a += got_a2[lax.rem(y + other, 4)].astype(F32)
            total_b += got_b2[lax.rem(x + other, 4)].astype(F32)
        image_a = jnp.maximum(total_a + inject[:HALF], 0.0)
        image_b = jnp.maximum(total_b + inject[HALF:], 0.0)
        images[k + 4, pl.ds(0, HALF)] = image_a
        images[k + 4, pl.ds(HALF, HALF)] = image_b
        residuals[k + 4, pl.ds(0, HALF)] = image_a - state[:HALF]
        residuals[k + 4, pl.ds(HALF, HALF)] = image_b - state[HALF:]
        for copy in copies:
            copy.wait_send()

        residual = residuals[k + 4]
        for pos in range(5):
            pack[pos : pos + 1, :] = lane_sums(residual, residuals[k + pos])
        head, tail = pack[0:8], pack[8:16]
        lanes = lax.broadcasted_iota(jnp.int32, (8, TILE), 1)
        own = jnp.where(lanes < 64, head + pltpu.roll(head, 64, 1), tail + pltpu.roll(tail, 64, 1))
        gram_send1[...] = own
        gram_got1[col] = own

        def gram1(step):
            to = lax.rem(col + step, 16)
            return pltpu.make_async_remote_copy(
                src_ref=gram_send1, dst_ref=gram_got1.at[col], send_sem=g1_send.at[step], recv_sem=g1_recv.at[col],
                device_id=(row, to), device_id_type=MESH,
            )

        def gram2(step):
            to = lax.rem(row + step, 16)
            return pltpu.make_async_remote_copy(
                src_ref=gram_send2, dst_ref=gram_got2.at[row], send_sem=g2_send.at[step], recv_sem=g2_recv.at[row],
                device_id=(to, col), device_id_type=MESH,
            )

        @pl.loop(1, 16)
        def _(step):
            gram1(step).start()

        @pl.loop(1, 16)
        def _(step):
            source = lax.rem(col + step, 16)
            pltpu.make_async_copy(gram_got1.at[source], gram_got1.at[source], g1_recv.at[source]).wait()

        own = jnp.sum(gram_got1[...], axis=0)
        gram_send2[...] = own
        gram_got2[row] = own

        @pl.loop(1, 16)
        def _(step):
            gram2(step).start()

        @pl.loop(1, 16)
        def _(step):
            source = lax.rem(row + step, 16)
            pltpu.make_async_copy(gram_got2.at[source], gram_got2.at[source], g2_recv.at[source]).wait()

        whole = jnp.sum(gram_got2[...], axis=0)
        head = jnp.sum(jnp.where(lanes < 64, whole, 0.0), axis=1, keepdims=True)
        tail = jnp.sum(jnp.where(lanes < 64, 0.0, whole), axis=1, keepdims=True)
        head = jnp.broadcast_to(head, (8, TILE))
        tail = jnp.broadcast_to(tail, (8, TILE))
        values = [head[pos : pos + 1] for pos in range(8)] + [tail[pos : pos + 1] for pos in range(8)]
        gram = {(4, pos): values[pos] for pos in range(5)}
        for pos, pair in enumerate(OLD_PAIRS):
            gram[pair] = values[5 + pos]
        alpha = mixing_weights(gram)
        alpha = [jnp.concatenate([value, value], axis=1) for value in alpha]
        mixed = alpha[0] * images[k]
        for pos in range(1, 5):
            mixed += alpha[pos] * images[k + pos]
        state[...] = mixed

        @pl.loop(1, 16)
        def _(step):
            gram1(step).wait_send()
            gram2(step).wait_send()

    state_out[...] = state[...]
    residual_out[...] = residuals[ITERS + 3]


def on_device(
    iterate,
    past_images,
    past_residuals,
    features,
    input_weight,
    mix_weight,
    tile_values,
    tile_rows,
    tile_cols,
    tile_count,
):
    dense = build_dense(tile_rows[0, 0], tile_cols[0, 0], tile_count[0], tile_values[0, 0])
    dma = pltpu.SemaphoreType.DMA
    vmem = pl.BlockSpec(memory_space=pltpu.VMEM)
    hbm = pl.BlockSpec(memory_space=pl.ANY)
    block = jax.ShapeDtypeStruct((TILE, CHANNELS), F32)
    quad = pltpu.VMEM((4, 4, HALF, CHANNELS), BF16)
    single = pltpu.VMEM((4, HALF, CHANNELS), BF16)
    return pl.pallas_call(
        main_kernel,
        out_shape=(block, block),
        in_specs=[vmem] * 4 + [hbm] * 3,
        out_specs=(vmem, vmem),
        scratch_shapes=[
            pltpu.VMEM((16, 16, TILE, TILE), BF16),
            pltpu.VMEM((16, TILE, CHANNELS), BF16),
            pltpu.VMEM((4, 4 * TILE, CHANNELS), F32),
            quad, quad, quad, quad, single, single, single, single,
            pltpu.VMEM((TILE, CHANNELS), F32),
            pltpu.VMEM((TILE, CHANNELS), F32),
            pltpu.VMEM((ITERS + 4, TILE, CHANNELS), F32),
            pltpu.VMEM((ITERS + 4, TILE, CHANNELS), F32),
            pltpu.VMEM((16, TILE), F32),
            pltpu.VMEM((8, TILE), F32),
            pltpu.VMEM((8, TILE), F32),
            pltpu.VMEM((16, 8, TILE), F32),
            pltpu.VMEM((16, 8, TILE), F32),
            dma((3,)), dma((16,)), dma((17,)),
            dma((4,)), dma((4,)), dma((4,)), dma((4,)), dma((4,)), dma((4,)), dma((4,)), dma((4,)),
            dma((16,)), dma((16,)), dma((16,)), dma((16,)),
        ],
        compiler_params=pltpu.CompilerParams(
            collective_id=0, has_side_effects=True, vmem_limit_bytes=40 * 1024 * 1024
        ),
        name="anderson",
    )(iterate, features, input_weight, mix_weight, past_images, past_residuals, dense)


def solution(mesh):
    return jax.shard_map(
        on_device,
        mesh=mesh,
        in_specs=(
            P(("row", "col"), None),
            P(None, ("row", "col"), None),
            P(None, ("row", "col"), None),
            P(("row", "col"), None),
            P(),
            P(),
            P("row", "col", None, None, None),
            P("row", "col", None),
            P("row", "col", None),
            P("row", "col"),
        ),
        out_specs=(P(("row", "col"), None), P(("row", "col"), None)),
        check_vma=False,
    )
```

```python
import jax
import jax.numpy as jnp
from jax import lax
from jax.experimental import pallas as pl
from jax.experimental.pallas import tpu as pltpu
from jax.sharding import PartitionSpec as P

ITERS = 3
TILE = 128
HALF = 64
CHANNELS = 256
MESH = pl.DeviceIdType.MESH
F32 = jnp.float32
BF16 = jnp.bfloat16
CHUNKS = 8
SLOTS = 256


def build_kernel(rows_hbm, cols_hbm, count_ref, values_ref, dense_ref, rows_ref, cols_ref, buf, acc, in_sem, index_sem):
    size = SLOTS // CHUNKS
    index_loads = [
        pltpu.make_async_copy(rows_hbm.at[0, 0], rows_ref, index_sem.at[0]),
        pltpu.make_async_copy(cols_hbm.at[0, 0], cols_ref, index_sem.at[1]),
    ]
    for load in index_loads:
        load.start()
    loads = []
    for chunk in range(CHUNKS):
        span = pl.ds(chunk * size, size)
        loads.append(pltpu.make_async_copy(values_ref.at[span], buf.at[span], in_sem.at[chunk]))
        loads[-1].start()
    count = count_ref[0]

    @pl.loop(0, 256, unroll=8)
    def _(cell):
        acc[cell] = jnp.zeros((TILE, TILE), F32)

    for load in index_loads:
        load.wait()
    for chunk in range(CHUNKS):
        loads[chunk].wait()

        @pl.loop(chunk * size, jnp.minimum(count, (chunk + 1) * size))
        def _(slot):
            cell = cols_ref[slot] * 16 + rows_ref[slot]
            acc[cell] += buf[slot].astype(F32)

    @pl.loop(0, 256, unroll=8)
    def _(cell):
        dense_ref[cell] = acc[cell].astype(BF16)


def build_dense(rows, cols, count, values):
    hbm = pl.BlockSpec(memory_space=pltpu.HBM)
    return pl.pallas_call(
        build_kernel,
        out_shape=jax.ShapeDtypeStruct((256, TILE, TILE), BF16),
        in_specs=[hbm, hbm, pl.BlockSpec(memory_space=pltpu.SMEM), hbm],
        out_specs=pl.BlockSpec(memory_space=pltpu.VMEM),
        scratch_shapes=[
            pltpu.SMEM((SLOTS,), jnp.int32),
            pltpu.SMEM((SLOTS,), jnp.int32),
            pltpu.VMEM((SLOTS, TILE, TILE), BF16),
            pltpu.VMEM((256, TILE, TILE), F32),
            pltpu.SemaphoreType.DMA((CHUNKS,)),
            pltpu.SemaphoreType.DMA((2,)),
        ],
        compiler_params=pltpu.CompilerParams(vmem_limit_bytes=40 * 1024 * 1024),
        name="build_dense",
    )(rows, cols, count, values)


def mixing_weights(gram):
    trace = gram[0, 0]
    for pos in range(1, 5):
        trace = trace + gram[pos, pos]
    shift = 0.05 * (trace / 5.0)
    lower = {}
    for first in range(5):
        for second in range(first + 1):
            total = gram[first, second]
            if first == second:
                total = total + shift
            for inner in range(second):
                total = total - lower[first, inner] * lower[second, inner]
            if first == second:
                lower[first, second] = jnp.sqrt(total)
            else:
                lower[first, second] = total / lower[second, second]
    forward = []
    for first in range(5):
        total = jnp.ones_like(trace)
        for inner in range(first):
            total = total - lower[first, inner] * forward[inner]
        forward.append(total / lower[first, first])
    backward = [None] * 5
    for first in reversed(range(5)):
        total = forward[first]
        for inner in range(first + 1, 5):
            total = total - lower[inner, first] * backward[inner]
        backward[first] = total / lower[first, first]
    norm = backward[0]
    for pos in range(1, 5):
        norm = norm + backward[pos]
    return [value / norm for value in backward]


OLD_PAIRS = [(first, second) for first in range(4) for second in range(first + 1)]


def lane_sums(left, right):
    return jnp.sum(left * right, axis=0, keepdims=True)


def main_kernel(
    iterate_ref, features_ref, input_weight_ref, mix_weight_ref, past_images_ref, past_residuals_ref, dense,
    state_out, residual_out,
    panel, acc, part, got1, sums, got2,
    state, inject, images, residuals, pack, gram_send1, gram_send2, gram_got1, gram_got2,
    load_sem, ag_send, ag_recv, rs1_send, rs1_recv, rs2_send, rs2_recv, gram_sem,
):
    row = lax.axis_index("row")
    col = lax.axis_index("col")
    z, core = row // 2, lax.rem(row, 2)
    y, x = col // 4, lax.rem(col, 4)
    first_axis, second_axis = (x, y), (y, x)
    sibling = row + 1 - 2 * core

    loads = []
    for half in range(2):
        for past_ref, kept in ((past_images_ref, images), (past_residuals_ref, residuals)):
            source = past_ref.at[pl.ds(1, 4), :, pl.ds(half * TILE, TILE)]
            loads.append(pltpu.make_async_copy(source, kept.at[pl.ds(0, 4), half], load_sem.at[len(loads)]))
            loads[-1].start()

    barrier = pltpu.get_barrier_semaphore()

    @pl.loop(1, 16)
    def _(step):
        pl.semaphore_signal(barrier, inc=1, device_id=(row, lax.rem(col + step, 16)), device_id_type=MESH)
        pl.semaphore_signal(barrier, inc=1, device_id=(lax.rem(row + step, 16), col), device_id_type=MESH)

    state[...] = iterate_ref[...]
    inject[...] = jnp.dot(features_ref[...], input_weight_ref[...], preferred_element_type=F32)
    pack[...] = jnp.zeros_like(pack)
    pl.semaphore_wait(barrier, 30)

    def chip(offset):
        return lax.rem(z + offset + 8, 8)

    def own_tile(offset):
        return 2 * chip(offset) + core

    def twin_tile(offset):
        return 2 * chip(offset) + 1 - core

    def gather_send(half, ref, target, slot, recv):
        return pltpu.make_async_remote_copy(
            src_ref=ref,
            dst_ref=ref,
            send_sem=ag_send.at[half, slot],
            recv_sem=ag_recv.at[half, recv],
            device_id=(target, col),
            device_id_type=MESH,
        )

    def gather_wait(half, tile, part=None, recv=None):
        ref = panel.at[half, tile] if part is None else panel.at[half, tile, part]
        pltpu.make_async_copy(ref, ref, ag_recv.at[half, tile if recv is None else recv]).wait()

    def multiply(half, spots, first=False, last=False):
        rhs = jnp.concatenate([panel[half, 2 * spot + side] for spot in spots for side in range(2)], axis=0)
        lhs = [dense[pl.ds(16 * (2 * spot + side), 16)].reshape(16 * TILE, TILE) for spot in spots for side in range(2)]
        product = jnp.dot(jnp.concatenate(lhs, axis=1), rhs, preferred_element_type=F32)
        if first:
            acc[half] = product
        elif not last:
            acc[half] += product
        else:
            total = (acc[half] + product).astype(BF16)
            for tile in range(16):
                tile_y, tile_x = tile // 4, tile % 4
                part[half, 0, tile_x, tile_y] = total[tile * TILE : tile * TILE + HALF]
                part[half, 1, tile_y, tile_x] = total[tile * TILE + HALF : (tile + 1) * TILE]

    def all_waits(ref, sem):
        pltpu.make_async_copy(ref, ref, sem).wait()

    def scatter1(half, way, step):
        to = lax.rem(first_axis[way] + step, 4)
        return pltpu.make_async_remote_copy(
            src_ref=part.at[half, way, to], dst_ref=got1.at[half, way, first_axis[way]],
            send_sem=rs1_send.at[half, way], recv_sem=rs1_recv.at[half, way],
            device_id=(row, 4 * y + to if way == 0 else 4 * to + x), device_id_type=MESH,
        )

    def scatter2(half, way, step):
        to = lax.rem(second_axis[way] + step, 4)
        return pltpu.make_async_remote_copy(
            src_ref=sums.at[half, way, to], dst_ref=got2.at[half, way, second_axis[way]],
            send_sem=rs2_send.at[half, way], recv_sem=rs2_recv.at[half, way],
            device_id=(row, 4 * to + x if way == 0 else 4 * y + to), device_id_type=MESH,
        )

    def gram1(step):
        to = lax.rem(col + step, 16)
        return pltpu.make_async_remote_copy(
            src_ref=gram_send1, dst_ref=gram_got1.at[col], send_sem=gram_sem.at[0], recv_sem=gram_sem.at[1],
            device_id=(row, to), device_id_type=MESH,
        )

    def gram2(step):
        to = lax.rem(row + step, 16)
        return pltpu.make_async_remote_copy(
            src_ref=gram_send2, dst_ref=gram_got2.at[row], send_sem=gram_sem.at[2], recv_sem=gram_sem.at[3],
            device_id=(to, col), device_id_type=MESH,
        )

    @pl.loop(0, ITERS)
    def _(k):
        message = jnp.dot(state[...].astype(BF16), mix_weight_ref[...], preferred_element_type=F32).astype(BF16)
        sends = []
        used = [0, 0]

        def send(half, tile, target, part=None, recv=None):
            ref = panel.at[half, tile] if part is None else panel.at[half, tile, part]
            sends.append(gather_send(half, ref, target, used[half], tile if recv is None else recv))
            sends[-1].start()
            used[half] += 1

        for half in range(2):
            panel[half, row] = message[:, half * TILE : (half + 1) * TILE]
            for offset in (2, -2, 0, 1, -1):
                send(half, row, sibling if offset == 0 else own_tile(offset))

        @pl.when(k == 0)
        def _():
            for load in loads:
                load.wait()

        for pos, (first, second) in enumerate(OLD_PAIRS):
            pack[5 + pos : 6 + pos, :] = sum(lane_sums(residuals[k + first, half], residuals[k + second, half]) for half in range(2))

        low, high = pl.ds(0, TILE // 2), pl.ds(TILE // 2, TILE // 2)

        def near(half):
            for sign, part, extra in ((-1, low, None), (1, high, 16)):
                tile = own_tile(2 * sign)
                gather_wait(half, tile)
                send(half, tile, own_tile(-2 * sign), part, tile if extra is None else extra)
                send(half, tile, own_tile(-sign))
                send(half, tile, sibling)
            for sign in (-1, 1):
                gather_wait(half, own_tile(sign))
                send(half, own_tile(sign), sibling)

        def product(half, *offsets, **where):
            for offset in offsets:
                gather_wait(half, twin_tile(offset))
            multiply(half, [chip(offset) for offset in offsets], **where)

        def distant(half):
            for offset in (-3, 3):
                gather_wait(half, own_tile(offset))
                send(half, own_tile(offset), sibling)
            gather_wait(half, own_tile(4), low)
            gather_wait(half, own_tile(4), high, 16)
            send(half, own_tile(4), sibling)

        def scatter(half):
            for step in (2, 1, 3):
                for way in range(2):
                    scatter1(half, way, step).start()

        near(0)
        product(0, 0, first=True)
        near(1)
        product(0, 1, -1)
        product(0, 2, -2)
        product(1, 0, first=True)
        distant(0)
        product(1, 1, -1)
        product(0, 3, -3)
        product(0, 4, last=True)
        scatter(0)
        distant(1)
        product(1, 2, -2)
        product(1, 3, -3)
        product(1, 4, last=True)
        scatter(1)

        for half in range(2):
            for way in range(2):
                all_waits(got1.at[half, way, pl.ds(0, 3)], rs1_recv.at[half, way])
                total = part[half, way, first_axis[way]].astype(F32)
                for step in range(1, 4):
                    total += got1[half, way, lax.rem(first_axis[way] + step, 4)].astype(F32)
                sums[half, way] = total.astype(BF16)
                for step in (2, 1, 3):
                    scatter2(half, way, step).start()

        scores = [0.0] * 5
        for half in range(2):
            lanes = slice(half * TILE, (half + 1) * TILE)
            for way in range(2):
                rows = slice(way * HALF, (way + 1) * HALF)
                all_waits(got2.at[half, way, pl.ds(0, 3)], rs2_recv.at[half, way])
                total = sums[half, way, second_axis[way]].astype(F32)
                for step in range(1, 4):
                    total += got2[half, way, lax.rem(second_axis[way] + step, 4)].astype(F32)
                image = jnp.maximum(total + inject[rows, lanes], 0.0)
                residual = image - state[rows, lanes]
                images[k + 4, half, rows] = image
                residuals[k + 4, half, rows] = residual
                for pos in range(5):
                    other = residual if pos == 4 else residuals[k + pos, half, rows]
                    scores[pos] = scores[pos] + lane_sums(residual, other)

        for pos in range(5):
            pack[pos : pos + 1, :] = scores[pos]
        head, tail = pack[0:8], pack[8:16]
        lanes = lax.broadcasted_iota(jnp.int32, (8, TILE), 1)
        own = jnp.where(lanes < 64, head + pltpu.roll(head, 64, 1), tail + pltpu.roll(tail, 64, 1))
        gram_send1[...] = own
        gram_got1[col] = own

        @pl.loop(1, 16, unroll=5)
        def _(step):
            gram1(step).start()

        for copy in sends:
            copy.wait_send()

        for half in range(2):
            for way in range(2):
                all_waits(part.at[half, way, pl.ds(0, 3)], rs1_send.at[half, way])
                all_waits(sums.at[half, way, pl.ds(0, 3)], rs2_send.at[half, way])
        all_waits(gram_got1.at[pl.ds(0, 15)], gram_sem.at[1])

        own = jnp.sum(gram_got1[...], axis=0)
        gram_send2[...] = own
        gram_got2[row] = own

        @pl.loop(1, 16, unroll=5)
        def _(step):
            gram2(step).start()

        all_waits(gram_got2.at[pl.ds(0, 15)], gram_sem.at[3])

        whole = jnp.sum(gram_got2[...], axis=0)
        head = jnp.sum(jnp.where(lanes < 64, whole, 0.0), axis=1, keepdims=True)
        tail = jnp.sum(jnp.where(lanes < 64, 0.0, whole), axis=1, keepdims=True)
        head = jnp.broadcast_to(head, (8, TILE))
        tail = jnp.broadcast_to(tail, (8, TILE))
        values = [head[pos : pos + 1] for pos in range(8)] + [tail[pos : pos + 1] for pos in range(8)]
        gram = {(4, pos): values[pos] for pos in range(5)}
        for pos, pair in enumerate(OLD_PAIRS):
            gram[pair] = values[5 + pos]
        alpha = mixing_weights(gram)
        for half in range(2):
            mixed = alpha[0] * images[k, half]
            for pos in range(1, 5):
                mixed += alpha[pos] * images[k + pos, half]
            state[:, half * TILE : (half + 1) * TILE] = mixed

        all_waits(gram_got1.at[pl.ds(0, 15)], gram_sem.at[0])
        all_waits(gram_got2.at[pl.ds(0, 15)], gram_sem.at[2])

    state_out[...] = state[...]
    for half in range(2):
        residual_out[:, half * TILE : (half + 1) * TILE] = residuals[ITERS + 3, half]


def on_device(
    iterate,
    past_images,
    past_residuals,
    features,
    input_weight,
    mix_weight,
    tile_values,
    tile_rows,
    tile_cols,
    tile_count,
):
    dense = build_dense(tile_rows, tile_cols, tile_count[0], tile_values[0, 0])
    dma = pltpu.SemaphoreType.DMA
    vmem = pl.BlockSpec(memory_space=pltpu.VMEM)
    hbm = pl.BlockSpec(memory_space=pl.ANY)
    block = jax.ShapeDtypeStruct((TILE, CHANNELS), F32)
    history = pltpu.VMEM((ITERS + 4, 2, TILE, TILE), F32)
    quads = pltpu.VMEM((2, 2, 4, 4, HALF, TILE), BF16)
    singles = pltpu.VMEM((2, 2, 4, HALF, TILE), BF16)
    return pl.pallas_call(
        main_kernel,
        out_shape=(block, block),
        in_specs=[vmem] * 4 + [hbm] * 2 + [vmem],
        out_specs=(vmem, vmem),
        scratch_shapes=[
            pltpu.VMEM((2, 16, TILE, TILE), BF16),
            pltpu.VMEM((2, 16 * TILE, TILE), F32),
            quads, quads, singles, singles,
            pltpu.VMEM((TILE, CHANNELS), F32),
            pltpu.VMEM((TILE, CHANNELS), F32),
            history,
            history,
            pltpu.VMEM((16, TILE), F32),
            pltpu.VMEM((8, TILE), F32),
            pltpu.VMEM((8, TILE), F32),
            pltpu.VMEM((16, 8, TILE), F32),
            pltpu.VMEM((16, 8, TILE), F32),
            dma((4,)), dma((2, 16)), dma((2, 17)), dma((2, 2)), dma((2, 2)), dma((2, 2)), dma((2, 2)), dma((4,)),
        ],
        compiler_params=pltpu.CompilerParams(
            collective_id=0, has_side_effects=True, vmem_limit_bytes=24 * 1024 * 1024
        ),
        name="anderson",
    )(iterate, features, input_weight, mix_weight, past_images, past_residuals, dense)


def solution(mesh):
    return jax.shard_map(
        on_device,
        mesh=mesh,
        in_specs=(
            P(("row", "col"), None),
            P(None, ("row", "col"), None),
            P(None, ("row", "col"), None),
            P(("row", "col"), None),
            P(),
            P(),
            P("row", "col", None, None, None),
            P("row", "col", None),
            P("row", "col", None),
            P("row", "col"),
        ),
        out_specs=(P(("row", "col"), None), P(("row", "col"), None)),
        check_vma=False,
    )
```

```python
import jax
import jax.numpy as jnp
from jax import lax
from jax.experimental import pallas as pl
from jax.experimental.pallas import tpu as pltpu
from jax.sharding import PartitionSpec as P

ITERS = 3
TILE = 128
HALF = 64
CHANNELS = 256
MESH = pl.DeviceIdType.MESH
F32 = jnp.float32
BF16 = jnp.bfloat16
CHUNKS = 8
SLOTS = 256


def build_kernel(cells_ref, count_ref, values_ref, dense_ref, buf, acc, in_sem):
    size = SLOTS // CHUNKS
    loads = []
    for chunk in range(CHUNKS):
        span = pl.ds(chunk * size, size)
        loads.append(pltpu.make_async_copy(values_ref.at[span], buf.at[span], in_sem.at[chunk]))
        loads[-1].start()
    count = count_ref[0]

    @pl.loop(0, 256, unroll=8)
    def _(cell):
        acc[cell] = jnp.zeros((TILE, TILE), F32)

    for chunk in range(CHUNKS):
        loads[chunk].wait()

        @pl.loop(chunk * size, jnp.minimum(count, (chunk + 1) * size))
        def _(slot):
            acc[cells_ref[slot]] += buf[slot].astype(F32)

    @pl.loop(0, 256, unroll=8)
    def _(cell):
        dense_ref[cell] = acc[cell].astype(BF16)


def build_dense(cells, count, values):
    smem = pl.BlockSpec(memory_space=pltpu.SMEM)
    return pl.pallas_call(
        build_kernel,
        out_shape=jax.ShapeDtypeStruct((256, TILE, TILE), BF16),
        in_specs=[smem, smem, pl.BlockSpec(memory_space=pl.ANY)],
        out_specs=pl.BlockSpec(memory_space=pltpu.VMEM),
        scratch_shapes=[
            pltpu.VMEM((SLOTS, TILE, TILE), BF16),
            pltpu.VMEM((256, TILE, TILE), F32),
            pltpu.SemaphoreType.DMA((CHUNKS,)),
        ],
        compiler_params=pltpu.CompilerParams(vmem_limit_bytes=40 * 1024 * 1024),
        name="build_dense",
    )(cells, count, values)


def mixing_weights(gram):
    trace = gram[0, 0]
    for pos in range(1, 5):
        trace = trace + gram[pos, pos]
    shift = 0.05 * (trace / 5.0)
    left = dict(gram)
    for pos in range(5):
        left[pos, pos] = left[pos, pos] + shift
    right = [jnp.ones_like(trace)] * 5
    inverse = []
    for pivot in range(5):
        inverse.append(1.0 / left[pivot, pivot])
        for first in range(pivot + 1, 5):
            factor = left[first, pivot] * inverse[pivot]
            for second in range(pivot + 1, first + 1):
                left[first, second] = left[first, second] - factor * left[second, pivot]
            right[first] = right[first] - factor * right[pivot]
    weights = [None] * 5
    for first in reversed(range(5)):
        total = right[first]
        for inner in range(first + 1, 5):
            total = total - left[inner, first] * weights[inner]
        weights[first] = total * inverse[first]
    norm = weights[0]
    for pos in range(1, 5):
        norm = norm + weights[pos]
    scale = 1.0 / norm
    return [value * scale for value in weights]


OLD_PAIRS = [(first, second) for first in range(4) for second in range(first + 1)]


FAR_COL = sorted(
    [(over_y, over_x) for over_y in range(4) for over_x in range(4)][1:],
    key=lambda over: -sum(min(step, 4 - step) for step in over),
)
FAR_ROW = sorted(
    [(over_z, over_core) for over_z in range(8) for over_core in range(2)][1:],
    key=lambda over: -min(over[0], 8 - over[0]),
)


def lane_sums(left, right):
    return jnp.sum(left * right, axis=0, keepdims=True)


def main_kernel(
    iterate_ref, features_ref, input_weight_ref, mix_weight_ref, past_images_ref, past_residuals_ref, dense,
    state_out, residual_out,
    panel, acc, part, got1, sums, got2,
    state, inject, images, residuals, pack, gram_send1, gram_send2, gram_got1, gram_got2,
    load_sem, ag_send, ag_recv, rs1_send, rs1_recv, rs2_send, rs2_recv, gram_sem,
):
    row = lax.axis_index("row")
    col = lax.axis_index("col")
    z, core = row // 2, lax.rem(row, 2)
    y, x = col // 4, lax.rem(col, 4)
    first_axis, second_axis = (x, y), (y, x)
    sibling = row + 1 - 2 * core

    loads = []
    for half in range(2):
        for past_ref, kept in ((past_images_ref, images), (past_residuals_ref, residuals)):
            source = past_ref.at[pl.ds(1, 4), :, pl.ds(half * TILE, TILE)]
            loads.append(pltpu.make_async_copy(source, kept.at[pl.ds(0, 4), half], load_sem.at[len(loads)]))
            loads[-1].start()

    barrier = pltpu.get_barrier_semaphore()

    @pl.loop(1, 16)
    def _(step):
        pl.semaphore_signal(barrier, inc=1, device_id=(row, lax.rem(col + step, 16)), device_id_type=MESH)
        pl.semaphore_signal(barrier, inc=1, device_id=(lax.rem(row + step, 16), col), device_id_type=MESH)

    state[...] = iterate_ref[...]
    inject[...] = jnp.dot(features_ref[...], input_weight_ref[...], preferred_element_type=F32)
    pack[...] = jnp.zeros_like(pack)
    pl.semaphore_wait(barrier, 30)

    def chip(offset):
        return lax.rem(z + offset + 8, 8)

    def own_tile(offset):
        return 2 * chip(offset) + core

    def twin_tile(offset):
        return 2 * chip(offset) + 1 - core

    def gather_send(half, ref, target, slot, recv):
        return pltpu.make_async_remote_copy(
            src_ref=ref,
            dst_ref=ref,
            send_sem=ag_send.at[half, slot],
            recv_sem=ag_recv.at[half, recv],
            device_id=(target, col),
            device_id_type=MESH,
        )

    def gather_wait(half, tile, part=None, recv=None):
        ref = panel.at[half, tile] if part is None else panel.at[half, tile, part]
        pltpu.make_async_copy(ref, ref, ag_recv.at[half, tile if recv is None else recv]).wait()

    def multiply(halves, spots, first=False, last=False):
        tiles = [2 * spot + side for spot in spots for side in range(2)]
        rhs = jnp.concatenate(
            [jnp.concatenate([panel[half, tile] for tile in tiles], axis=0) for half in halves], axis=1
        )
        lhs = jnp.concatenate([dense[pl.ds(16 * tile, 16)].reshape(16 * TILE, TILE) for tile in tiles], axis=1)
        product = jnp.dot(lhs, rhs, preferred_element_type=F32)
        for pos, half in enumerate(halves):
            term = product[:, pos * TILE : (pos + 1) * TILE]
            if first:
                acc[half] = term
            elif not last:
                acc[half] += term
            else:
                total = (acc[half] + term).astype(BF16)
                for tile in range(16):
                    tile_y, tile_x = tile // 4, tile % 4
                    part[half, 0, tile_x, tile_y] = total[tile * TILE : tile * TILE + HALF]
                    part[half, 1, tile_y, tile_x] = total[tile * TILE + HALF : (tile + 1) * TILE]

    def all_waits(ref, sem):
        pltpu.make_async_copy(ref, ref, sem).wait()

    def scatter1(half, way, step):
        to = lax.rem(first_axis[way] + step, 4)
        return pltpu.make_async_remote_copy(
            src_ref=part.at[half, way, to], dst_ref=got1.at[half, way, first_axis[way]],
            send_sem=rs1_send.at[half, way], recv_sem=rs1_recv.at[half, way],
            device_id=(row, 4 * y + to if way == 0 else 4 * to + x), device_id_type=MESH,
        )

    def scatter2(half, way, step):
        to = lax.rem(second_axis[way] + step, 4)
        return pltpu.make_async_remote_copy(
            src_ref=sums.at[half, way, to], dst_ref=got2.at[half, way, second_axis[way]],
            send_sem=rs2_send.at[half, way], recv_sem=rs2_recv.at[half, way],
            device_id=(row, 4 * to + x if way == 0 else 4 * y + to), device_id_type=MESH,
        )

    def gram1(over_y, over_x):
        to = 4 * lax.rem(y + over_y, 4) + lax.rem(x + over_x, 4)
        return pltpu.make_async_remote_copy(
            src_ref=gram_send1, dst_ref=gram_got1.at[col], send_sem=gram_sem.at[0], recv_sem=gram_sem.at[1],
            device_id=(row, to), device_id_type=MESH,
        )

    def gram2(over_z, over_core):
        to = 2 * lax.rem(z + over_z, 8) + lax.rem(core + over_core, 2)
        return pltpu.make_async_remote_copy(
            src_ref=gram_send2, dst_ref=gram_got2.at[row], send_sem=gram_sem.at[2], recv_sem=gram_sem.at[3],
            device_id=(to, col), device_id_type=MESH,
        )

    @pl.loop(0, ITERS)
    def _(k):
        message = jnp.dot(state[...].astype(BF16), mix_weight_ref[...], preferred_element_type=F32).astype(BF16)
        sends = []
        used = [0, 0]

        def send(half, tile, target, part=None, recv=None):
            ref = panel.at[half, tile] if part is None else panel.at[half, tile, part]
            sends.append(gather_send(half, ref, target, used[half], tile if recv is None else recv))
            sends[-1].start()
            used[half] += 1

        for half in range(2):
            panel[half, row] = message[:, half * TILE : (half + 1) * TILE]
            for offset in (2, -2, 0, 1, -1):
                send(half, row, sibling if offset == 0 else own_tile(offset))

        @pl.when(k == 0)
        def _():
            for load in loads:
                load.wait()

        for pos, (first, second) in enumerate(OLD_PAIRS):
            pack[5 + pos : 6 + pos, :] = sum(lane_sums(residuals[k + first, half], residuals[k + second, half]) for half in range(2))

        low, high = pl.ds(0, TILE // 2), pl.ds(TILE // 2, TILE // 2)

        def near(half):
            for sign, part, extra in ((-1, low, None), (1, high, 16)):
                tile = own_tile(2 * sign)
                gather_wait(half, tile)
                send(half, tile, own_tile(-2 * sign), part, tile if extra is None else extra)
                send(half, tile, own_tile(-sign))
                send(half, tile, sibling)
            for sign in (-1, 1):
                gather_wait(half, own_tile(sign))
                send(half, own_tile(sign), sibling)

        def product(halves, *offsets, **where):
            for half in halves:
                for offset in offsets:
                    gather_wait(half, twin_tile(offset))
            multiply(halves, [chip(offset) for offset in offsets], **where)

        def distant(half):
            for offset in (-3, 3):
                gather_wait(half, own_tile(offset))
                send(half, own_tile(offset), sibling)
            gather_wait(half, own_tile(4), low)
            gather_wait(half, own_tile(4), high, 16)
            send(half, own_tile(4), sibling)

        def scatter(half):
            for step in (2, 1, 3):
                for way in range(2):
                    scatter1(half, way, step).start()

        near(0)
        near(1)
        product((0, 1), 0, first=True)
        product((0, 1), 1, -1)
        distant(0)
        product((0, 1), 2, -2)
        product((0,), 3, -3)
        product((0,), 4, last=True)
        scatter(0)
        distant(1)
        product((1,), 3, -3)
        product((1,), 4, last=True)
        scatter(1)

        for half in range(2):
            for way in range(2):
                all_waits(got1.at[half, way, pl.ds(0, 3)], rs1_recv.at[half, way])
                total = part[half, way, first_axis[way]].astype(F32)
                for step in range(1, 4):
                    total += got1[half, way, lax.rem(first_axis[way] + step, 4)].astype(F32)
                sums[half, way] = total.astype(BF16)
                for step in (2, 1, 3):
                    scatter2(half, way, step).start()

        scores = [0.0] * 5
        for half in range(2):
            lanes = slice(half * TILE, (half + 1) * TILE)
            for way in range(2):
                rows = slice(way * HALF, (way + 1) * HALF)
                all_waits(got2.at[half, way, pl.ds(0, 3)], rs2_recv.at[half, way])
                total = sums[half, way, second_axis[way]].astype(F32)
                for step in range(1, 4):
                    total += got2[half, way, lax.rem(second_axis[way] + step, 4)].astype(F32)
                image = jnp.maximum(total + inject[rows, lanes], 0.0)
                residual = image - state[rows, lanes]
                images[k + 4, half, rows] = image
                residuals[k + 4, half, rows] = residual
                for pos in range(5):
                    other = residual if pos == 4 else residuals[k + pos, half, rows]
                    scores[pos] = scores[pos] + lane_sums(residual, other)

        for pos in range(5):
            pack[pos : pos + 1, :] = scores[pos]
        head, tail = pack[0:8], pack[8:16]
        lanes = lax.broadcasted_iota(jnp.int32, (8, TILE), 1)
        own = jnp.where(lanes < 64, head + pltpu.roll(head, 64, 1), tail + pltpu.roll(tail, 64, 1))
        gram_send1[...] = own
        gram_got1[col] = own

        for over in FAR_COL:
            gram1(*over).start()

        for copy in sends:
            copy.wait_send()

        for half in range(2):
            for way in range(2):
                all_waits(part.at[half, way, pl.ds(0, 3)], rs1_send.at[half, way])
                all_waits(sums.at[half, way, pl.ds(0, 3)], rs2_send.at[half, way])
        all_waits(gram_got1.at[pl.ds(0, 15)], gram_sem.at[1])

        own = jnp.sum(gram_got1[...], axis=0)
        gram_send2[...] = own
        gram_got2[row] = own

        for over in FAR_ROW:
            gram2(*over).start()

        all_waits(gram_got2.at[pl.ds(0, 15)], gram_sem.at[3])

        whole = jnp.sum(gram_got2[...], axis=0)
        head = jnp.sum(jnp.where(lanes < 64, whole, 0.0), axis=1, keepdims=True)
        tail = jnp.sum(jnp.where(lanes < 64, 0.0, whole), axis=1, keepdims=True)
        head = jnp.broadcast_to(head, (8, TILE))
        tail = jnp.broadcast_to(tail, (8, TILE))
        values = [head[pos : pos + 1] for pos in range(8)] + [tail[pos : pos + 1] for pos in range(8)]
        gram = {(4, pos): values[pos] for pos in range(5)}
        for pos, pair in enumerate(OLD_PAIRS):
            gram[pair] = values[5 + pos]
        alpha = mixing_weights(gram)
        for half in range(2):
            mixed = alpha[0] * images[k, half]
            for pos in range(1, 5):
                mixed += alpha[pos] * images[k + pos, half]
            state[:, half * TILE : (half + 1) * TILE] = mixed

        all_waits(gram_got1.at[pl.ds(0, 15)], gram_sem.at[0])
        all_waits(gram_got2.at[pl.ds(0, 15)], gram_sem.at[2])

    state_out[...] = state[...]
    for half in range(2):
        residual_out[:, half * TILE : (half + 1) * TILE] = residuals[ITERS + 3, half]


def on_device(
    iterate,
    past_images,
    past_residuals,
    features,
    input_weight,
    mix_weight,
    tile_values,
    tile_rows,
    tile_cols,
    tile_count,
):
    dense = build_dense((tile_cols * 16 + tile_rows)[0, 0], tile_count[0], tile_values[0, 0])
    dma = pltpu.SemaphoreType.DMA
    vmem = pl.BlockSpec(memory_space=pltpu.VMEM)
    hbm = pl.BlockSpec(memory_space=pl.ANY)
    block = jax.ShapeDtypeStruct((TILE, CHANNELS), F32)
    history = pltpu.VMEM((ITERS + 4, 2, TILE, TILE), F32)
    quads = pltpu.VMEM((2, 2, 4, 4, HALF, TILE), BF16)
    singles = pltpu.VMEM((2, 2, 4, HALF, TILE), BF16)
    return pl.pallas_call(
        main_kernel,
        out_shape=(block, block),
        in_specs=[vmem] * 4 + [hbm] * 2 + [vmem],
        out_specs=(vmem, vmem),
        scratch_shapes=[
            pltpu.VMEM((2, 16, TILE, TILE), BF16),
            pltpu.VMEM((2, 16 * TILE, TILE), F32),
            quads, quads, singles, singles,
            pltpu.VMEM((TILE, CHANNELS), F32),
            pltpu.VMEM((TILE, CHANNELS), F32),
            history,
            history,
            pltpu.VMEM((16, TILE), F32),
            pltpu.VMEM((8, TILE), F32),
            pltpu.VMEM((8, TILE), F32),
            pltpu.VMEM((16, 8, TILE), F32),
            pltpu.VMEM((16, 8, TILE), F32),
            dma((4,)), dma((2, 16)), dma((2, 17)), dma((2, 2)), dma((2, 2)), dma((2, 2)), dma((2, 2)), dma((4,)),
        ],
        compiler_params=pltpu.CompilerParams(
            collective_id=0, has_side_effects=True, vmem_limit_bytes=24 * 1024 * 1024
        ),
        name="anderson",
    )(iterate, features, input_weight, mix_weight, past_images, past_residuals, dense)


def solution(mesh):
    return jax.shard_map(
        on_device,
        mesh=mesh,
        in_specs=(
            P(("row", "col"), None),
            P(None, ("row", "col"), None),
            P(None, ("row", "col"), None),
            P(("row", "col"), None),
            P(),
            P(),
            P("row", "col", None, None, None),
            P("row", "col", None),
            P("row", "col", None),
            P("row", "col"),
        ),
        out_specs=(P(("row", "col"), None), P(("row", "col"), None)),
        check_vma=False,
    )
```

```python
import jax
import jax.numpy as jnp
from jax import lax
from jax.experimental import pallas as pl
from jax.experimental.pallas import tpu as pltpu
from jax.sharding import PartitionSpec as P

ITERS = 3
TILE = 128
HALF = 64
CHANNELS = 256
MESH = pl.DeviceIdType.MESH
F32 = jnp.float32
BF16 = jnp.bfloat16
CHUNKS = 8
SLOTS = 256


def build_kernel(cells_ref, count_ref, values_ref, dense_ref, buf, acc, in_sem):
    size = SLOTS // CHUNKS
    loads = []
    for chunk in range(CHUNKS):
        span = pl.ds(chunk * size, size)
        loads.append(pltpu.make_async_copy(values_ref.at[span], buf.at[span], in_sem.at[chunk]))
        loads[-1].start()
    count = count_ref[0]

    @pl.loop(0, 256, unroll=8)
    def _(cell):
        acc[cell] = jnp.zeros((TILE, TILE), F32)

    for chunk in range(CHUNKS):
        loads[chunk].wait()

        @pl.loop(chunk * size, jnp.minimum(count, (chunk + 1) * size))
        def _(slot):
            acc[cells_ref[slot]] += buf[slot].astype(F32)

    @pl.loop(0, 256, unroll=8)
    def _(cell):
        dense_ref[cell] = acc[cell].astype(BF16)


def build_dense(cells, count, values):
    smem = pl.BlockSpec(memory_space=pltpu.SMEM)
    return pl.pallas_call(
        build_kernel,
        out_shape=jax.ShapeDtypeStruct((256, TILE, TILE), BF16),
        in_specs=[smem, smem, pl.BlockSpec(memory_space=pl.ANY)],
        out_specs=pl.BlockSpec(memory_space=pltpu.VMEM),
        scratch_shapes=[
            pltpu.VMEM((SLOTS, TILE, TILE), BF16),
            pltpu.VMEM((256, TILE, TILE), F32),
            pltpu.SemaphoreType.DMA((CHUNKS,)),
        ],
        compiler_params=pltpu.CompilerParams(vmem_limit_bytes=40 * 1024 * 1024),
        name="build_dense",
    )(cells, count, values)


def mixing_weights(gram):
    trace = gram[0, 0]
    for pos in range(1, 5):
        trace = trace + gram[pos, pos]
    shift = 0.05 * (trace / 5.0)
    left = dict(gram)
    for pos in range(5):
        left[pos, pos] = left[pos, pos] + shift
    right = [jnp.ones_like(trace)] * 5
    inverse = []
    for pivot in range(5):
        inverse.append(1.0 / left[pivot, pivot])
        for first in range(pivot + 1, 5):
            factor = left[first, pivot] * inverse[pivot]
            for second in range(pivot + 1, first + 1):
                left[first, second] = left[first, second] - factor * left[second, pivot]
            right[first] = right[first] - factor * right[pivot]
    weights = [None] * 5
    for first in reversed(range(5)):
        total = right[first]
        for inner in range(first + 1, 5):
            total = total - left[inner, first] * weights[inner]
        weights[first] = total * inverse[first]
    norm = weights[0]
    for pos in range(1, 5):
        norm = norm + weights[pos]
    scale = 1.0 / norm
    return [value * scale for value in weights]


OLD_PAIRS = [(first, second) for first in range(4) for second in range(first + 1)]


FAR_COL = sorted(
    [(over_y, over_x) for over_y in range(4) for over_x in range(4)][1:],
    key=lambda over: -sum(min(step, 4 - step) for step in over),
)
FAR_ROW = sorted(
    [(over_z, over_core) for over_z in range(8) for over_core in range(2)][1:],
    key=lambda over: -min(over[0], 8 - over[0]),
)


def lane_sums(left, right):
    return jnp.sum(left * right, axis=0, keepdims=True)


def main_kernel(
    iterate_ref, features_ref, input_weight_ref, mix_weight_ref, past_images_ref, past_residuals_ref, dense,
    state_out, residual_out,
    panel, acc, part, got1, sums, got2,
    state, inject, images, residuals, pack, gram_send1, gram_send2, gram_got1, gram_got2,
    load_sem, ag_send, ag_recv, rs1_send, rs1_recv, rs2_send, rs2_recv, gram_sem,
):
    row = lax.axis_index("row")
    col = lax.axis_index("col")
    z, core = row // 2, lax.rem(row, 2)
    y, x = col // 4, lax.rem(col, 4)
    first_axis, second_axis = (x, y), (y, x)
    sibling = row + 1 - 2 * core

    barrier = pltpu.get_barrier_semaphore()
    for (over_y, over_x), (over_z, over_core) in zip(FAR_COL, FAR_ROW):
        to_col = 4 * lax.rem(y + over_y, 4) + lax.rem(x + over_x, 4)
        to_row = 2 * lax.rem(z + over_z, 8) + lax.rem(core + over_core, 2)
        pl.semaphore_signal(barrier, inc=1, device_id=(row, to_col), device_id_type=MESH)
        pl.semaphore_signal(barrier, inc=1, device_id=(to_row, col), device_id_type=MESH)

    loads = []
    for half in range(2):
        for past_ref, kept in ((past_images_ref, images), (past_residuals_ref, residuals)):
            source = past_ref.at[pl.ds(1, 4), :, pl.ds(half * TILE, TILE)]
            loads.append(pltpu.make_async_copy(source, kept.at[pl.ds(0, 4), half], load_sem.at[len(loads)]))
            loads[-1].start()

    state[...] = iterate_ref[...]
    inject[...] = jnp.dot(features_ref[...], input_weight_ref[...], preferred_element_type=F32)
    pack[...] = jnp.zeros_like(pack)
    pl.semaphore_wait(barrier, 30)

    def chip(offset):
        return lax.rem(z + offset + 8, 8)

    def own_tile(offset):
        return 2 * chip(offset) + core

    def twin_tile(offset):
        return 2 * chip(offset) + 1 - core

    def gather_send(half, ref, target, slot, recv):
        return pltpu.make_async_remote_copy(
            src_ref=ref,
            dst_ref=ref,
            send_sem=ag_send.at[half, slot],
            recv_sem=ag_recv.at[half, recv],
            device_id=(target, col),
            device_id_type=MESH,
        )

    def gather_wait(half, tile, part=None, recv=None):
        ref = panel.at[half, tile] if part is None else panel.at[half, tile, part]
        pltpu.make_async_copy(ref, ref, ag_recv.at[half, tile if recv is None else recv]).wait()

    def multiply(halves, spots, first=False, last=False):
        tiles = [2 * spot + side for spot in spots for side in range(2)]
        rhs = jnp.concatenate(
            [jnp.concatenate([panel[half, tile] for tile in tiles], axis=0) for half in halves], axis=1
        )
        lhs = jnp.concatenate([dense[pl.ds(16 * tile, 16)].reshape(16 * TILE, TILE) for tile in tiles], axis=1)
        product = jnp.dot(lhs, rhs, preferred_element_type=F32)
        for pos, half in enumerate(halves):
            term = product[:, pos * TILE : (pos + 1) * TILE]
            if first:
                acc[half] = term
            elif not last:
                acc[half] += term
            else:
                total = (acc[half] + term).astype(BF16)
                for tile in range(16):
                    tile_y, tile_x = tile // 4, tile % 4
                    part[half, 0, tile_x, tile_y] = total[tile * TILE : tile * TILE + HALF]
                    part[half, 1, tile_y, tile_x] = total[tile * TILE + HALF : (tile + 1) * TILE]

    def all_waits(ref, sem):
        pltpu.make_async_copy(ref, ref, sem).wait()

    def scatter1(half, way, step):
        to = lax.rem(first_axis[way] + step, 4)
        return pltpu.make_async_remote_copy(
            src_ref=part.at[half, way, to], dst_ref=got1.at[half, way, first_axis[way]],
            send_sem=rs1_send.at[half, way], recv_sem=rs1_recv.at[half, way],
            device_id=(row, 4 * y + to if way == 0 else 4 * to + x), device_id_type=MESH,
        )

    def scatter2(half, way, step):
        to = lax.rem(second_axis[way] + step, 4)
        return pltpu.make_async_remote_copy(
            src_ref=sums.at[half, way, to], dst_ref=got2.at[half, way, second_axis[way]],
            send_sem=rs2_send.at[half, way], recv_sem=rs2_recv.at[half, way],
            device_id=(row, 4 * to + x if way == 0 else 4 * y + to), device_id_type=MESH,
        )

    def gram1(over_y, over_x):
        to = 4 * lax.rem(y + over_y, 4) + lax.rem(x + over_x, 4)
        return pltpu.make_async_remote_copy(
            src_ref=gram_send1, dst_ref=gram_got1.at[col], send_sem=gram_sem.at[0], recv_sem=gram_sem.at[1],
            device_id=(row, to), device_id_type=MESH,
        )

    def gram2(over_z, over_core):
        to = 2 * lax.rem(z + over_z, 8) + lax.rem(core + over_core, 2)
        return pltpu.make_async_remote_copy(
            src_ref=gram_send2, dst_ref=gram_got2.at[row], send_sem=gram_sem.at[2], recv_sem=gram_sem.at[3],
            device_id=(to, col), device_id_type=MESH,
        )

    @pl.loop(0, ITERS)
    def _(k):
        lowered = state[...].astype(BF16)
        sends = []
        used = [0, 0]

        def send(half, tile, target, part=None, recv=None):
            ref = panel.at[half, tile] if part is None else panel.at[half, tile, part]
            sends.append(gather_send(half, ref, target, used[half], tile if recv is None else recv))
            sends[-1].start()
            used[half] += 1

        for half in range(2):
            weight = mix_weight_ref[:, half * TILE : (half + 1) * TILE]
            panel[half, row] = jnp.dot(lowered, weight, preferred_element_type=F32).astype(BF16)
            for offset in (2, -2):
                send(half, row, own_tile(offset))
        for half in range(2):
            for offset in (1, -1, 0):
                send(half, row, sibling if offset == 0 else own_tile(offset))

        @pl.when(k == 0)
        def _():
            for load in loads:
                load.wait()

        for pos, (first, second) in enumerate(OLD_PAIRS):
            pack[5 + pos : 6 + pos, :] = sum(lane_sums(residuals[k + first, half], residuals[k + second, half]) for half in range(2))

        low, high = pl.ds(0, TILE // 2), pl.ds(TILE // 2, TILE // 2)

        def relay(half):
            for sign, part, extra in ((-1, low, None), (1, high, 16)):
                tile = own_tile(2 * sign)
                gather_wait(half, tile)
                send(half, tile, own_tile(-2 * sign), part, tile if extra is None else extra)
                send(half, tile, own_tile(-sign))
                send(half, tile, sibling)

        def adjacent(half):
            for sign in (-1, 1):
                gather_wait(half, own_tile(sign))
                send(half, own_tile(sign), sibling)

        def product(halves, *offsets, **where):
            for half in halves:
                for offset in offsets:
                    gather_wait(half, twin_tile(offset))
            multiply(halves, [chip(offset) for offset in offsets], **where)

        def distant(half):
            for offset in (-3, 3):
                gather_wait(half, own_tile(offset))
                send(half, own_tile(offset), sibling)
            gather_wait(half, own_tile(4), low)
            gather_wait(half, own_tile(4), high, 16)
            send(half, own_tile(4), sibling)

        def scatter(half):
            for step in (2, 1, 3):
                for way in range(2):
                    scatter1(half, way, step).start()

        relay(0)
        relay(1)
        adjacent(0)
        adjacent(1)
        product((0, 1), 0, first=True)
        product((0, 1), 1, -1)
        distant(0)
        distant(1)
        product((0, 1), 2, -2)
        product((0,), 3, -3)
        product((0,), 4, last=True)
        scatter(0)
        product((1,), 3, -3)
        product((1,), 4, last=True)
        scatter(1)

        for half in range(2):
            for way in range(2):
                all_waits(got1.at[half, way, pl.ds(0, 3)], rs1_recv.at[half, way])
                total = part[half, way, first_axis[way]].astype(F32)
                for step in range(1, 4):
                    total += got1[half, way, lax.rem(first_axis[way] + step, 4)].astype(F32)
                sums[half, way] = total.astype(BF16)
                for step in (2, 1, 3):
                    scatter2(half, way, step).start()

        scores = [0.0] * 5
        for half in range(2):
            lanes = slice(half * TILE, (half + 1) * TILE)
            for way in range(2):
                rows = slice(way * HALF, (way + 1) * HALF)
                all_waits(got2.at[half, way, pl.ds(0, 3)], rs2_recv.at[half, way])
                total = sums[half, way, second_axis[way]].astype(F32)
                for step in range(1, 4):
                    total += got2[half, way, lax.rem(second_axis[way] + step, 4)].astype(F32)
                image = jnp.maximum(total + inject[rows, lanes], 0.0)
                residual = image - state[rows, lanes]
                images[k + 4, half, rows] = image
                residuals[k + 4, half, rows] = residual
                for pos in range(5):
                    other = residual if pos == 4 else residuals[k + pos, half, rows]
                    scores[pos] = scores[pos] + lane_sums(residual, other)

        for pos in range(5):
            pack[pos : pos + 1, :] = scores[pos]
        head, tail = pack[0:8], pack[8:16]
        lanes = lax.broadcasted_iota(jnp.int32, (8, TILE), 1)
        own = jnp.where(lanes < 64, head + pltpu.roll(head, 64, 1), tail + pltpu.roll(tail, 64, 1))
        gram_send1[...] = own
        gram_got1[col] = own

        for over in FAR_COL:
            gram1(*over).start()

        for copy in sends:
            copy.wait_send()

        for half in range(2):
            for way in range(2):
                all_waits(part.at[half, way, pl.ds(0, 3)], rs1_send.at[half, way])
                all_waits(sums.at[half, way, pl.ds(0, 3)], rs2_send.at[half, way])
        all_waits(gram_got1.at[pl.ds(0, 15)], gram_sem.at[1])

        own = jnp.sum(gram_got1[...], axis=0)
        gram_send2[...] = own
        gram_got2[row] = own

        for over in FAR_ROW:
            gram2(*over).start()

        all_waits(gram_got2.at[pl.ds(0, 15)], gram_sem.at[3])

        whole = jnp.sum(gram_got2[...], axis=0)
        head = jnp.sum(jnp.where(lanes < 64, whole, 0.0), axis=1, keepdims=True)
        tail = jnp.sum(jnp.where(lanes < 64, 0.0, whole), axis=1, keepdims=True)
        head = jnp.broadcast_to(head, (8, TILE))
        tail = jnp.broadcast_to(tail, (8, TILE))
        values = [head[pos : pos + 1] for pos in range(8)] + [tail[pos : pos + 1] for pos in range(8)]
        gram = {(4, pos): values[pos] for pos in range(5)}
        for pos, pair in enumerate(OLD_PAIRS):
            gram[pair] = values[5 + pos]
        alpha = mixing_weights(gram)
        for half in range(2):
            mixed = alpha[0] * images[k, half]
            for pos in range(1, 5):
                mixed += alpha[pos] * images[k + pos, half]
            state[:, half * TILE : (half + 1) * TILE] = mixed

        all_waits(gram_got1.at[pl.ds(0, 15)], gram_sem.at[0])
        all_waits(gram_got2.at[pl.ds(0, 15)], gram_sem.at[2])

    state_out[...] = state[...]
    for half in range(2):
        residual_out[:, half * TILE : (half + 1) * TILE] = residuals[ITERS + 3, half]


def on_device(
    iterate,
    past_images,
    past_residuals,
    features,
    input_weight,
    mix_weight,
    tile_values,
    tile_rows,
    tile_cols,
    tile_count,
):
    dense = build_dense((tile_cols * 16 + tile_rows)[0, 0], tile_count[0], tile_values[0, 0])
    dma = pltpu.SemaphoreType.DMA
    vmem = pl.BlockSpec(memory_space=pltpu.VMEM)
    hbm = pl.BlockSpec(memory_space=pl.ANY)
    block = jax.ShapeDtypeStruct((TILE, CHANNELS), F32)
    history = pltpu.VMEM((ITERS + 4, 2, TILE, TILE), F32)
    quads = pltpu.VMEM((2, 2, 4, 4, HALF, TILE), BF16)
    singles = pltpu.VMEM((2, 2, 4, HALF, TILE), BF16)
    return pl.pallas_call(
        main_kernel,
        out_shape=(block, block),
        in_specs=[vmem] * 4 + [hbm] * 2 + [vmem],
        out_specs=(vmem, vmem),
        scratch_shapes=[
            pltpu.VMEM((2, 16, TILE, TILE), BF16),
            pltpu.VMEM((2, 16 * TILE, TILE), F32),
            quads, quads, singles, singles,
            pltpu.VMEM((TILE, CHANNELS), F32),
            pltpu.VMEM((TILE, CHANNELS), F32),
            history,
            history,
            pltpu.VMEM((16, TILE), F32),
            pltpu.VMEM((8, TILE), F32),
            pltpu.VMEM((8, TILE), F32),
            pltpu.VMEM((16, 8, TILE), F32),
            pltpu.VMEM((16, 8, TILE), F32),
            dma((4,)), dma((2, 16)), dma((2, 17)), dma((2, 2)), dma((2, 2)), dma((2, 2)), dma((2, 2)), dma((4,)),
        ],
        compiler_params=pltpu.CompilerParams(
            collective_id=0, has_side_effects=True, vmem_limit_bytes=24 * 1024 * 1024
        ),
        name="anderson",
    )(iterate, features, input_weight, mix_weight, past_images, past_residuals, dense)


def solution(mesh):
    return jax.shard_map(
        on_device,
        mesh=mesh,
        in_specs=(
            P(("row", "col"), None),
            P(None, ("row", "col"), None),
            P(None, ("row", "col"), None),
            P(("row", "col"), None),
            P(),
            P(),
            P("row", "col", None, None, None),
            P("row", "col", None),
            P("row", "col", None),
            P("row", "col"),
        ),
        out_specs=(P(("row", "col"), None), P(("row", "col"), None)),
        check_vma=False,
    )
```

```python
import jax
import jax.numpy as jnp
from jax import lax
from jax.experimental import pallas as pl
from jax.experimental.pallas import tpu as pltpu
from jax.sharding import PartitionSpec as P

ITERS = 3
TILE = 128
HALF = 64
CHANNELS = 256
MESH = pl.DeviceIdType.MESH
F32 = jnp.float32
BF16 = jnp.bfloat16
CHUNKS = 8
SLOTS = 256


def build_kernel(cells_ref, count_ref, values_ref, dense_ref, buf, acc, in_sem):
    size = SLOTS // CHUNKS
    loads = []
    for chunk in range(CHUNKS):
        span = pl.ds(chunk * size, size)
        loads.append(pltpu.make_async_copy(values_ref.at[span], buf.at[span], in_sem.at[chunk]))
        loads[-1].start()
    count = count_ref[0]

    @pl.loop(0, 256, unroll=8)
    def _(cell):
        acc[cell] = jnp.zeros((TILE, TILE), F32)

    for chunk in range(CHUNKS):
        loads[chunk].wait()

        @pl.loop(chunk * size, jnp.minimum(count, (chunk + 1) * size))
        def _(slot):
            acc[cells_ref[slot]] += buf[slot].astype(F32)

    @pl.loop(0, 256, unroll=8)
    def _(cell):
        dense_ref[cell] = acc[cell].astype(BF16)


def build_dense(cells, count, values):
    smem = pl.BlockSpec(memory_space=pltpu.SMEM)
    return pl.pallas_call(
        build_kernel,
        out_shape=jax.ShapeDtypeStruct((256, TILE, TILE), BF16),
        in_specs=[smem, smem, pl.BlockSpec(memory_space=pl.ANY)],
        out_specs=pl.BlockSpec(memory_space=pltpu.VMEM),
        scratch_shapes=[
            pltpu.VMEM((SLOTS, TILE, TILE), BF16),
            pltpu.VMEM((256, TILE, TILE), F32),
            pltpu.SemaphoreType.DMA((CHUNKS,)),
        ],
        compiler_params=pltpu.CompilerParams(vmem_limit_bytes=40 * 1024 * 1024),
        name="build_dense",
    )(cells, count, values)


def mixing_weights(gram):
    trace = gram[0, 0]
    for pos in range(1, 5):
        trace = trace + gram[pos, pos]
    shift = 0.05 * (trace / 5.0)
    left = dict(gram)
    for pos in range(5):
        left[pos, pos] = left[pos, pos] + shift
    right = [jnp.ones_like(trace)] * 5
    inverse = []
    for pivot in range(5):
        inverse.append(1.0 / left[pivot, pivot])
        for first in range(pivot + 1, 5):
            factor = left[first, pivot] * inverse[pivot]
            for second in range(pivot + 1, first + 1):
                left[first, second] = left[first, second] - factor * left[second, pivot]
            right[first] = right[first] - factor * right[pivot]
    weights = [None] * 5
    for first in reversed(range(5)):
        total = right[first]
        for inner in range(first + 1, 5):
            total = total - left[inner, first] * weights[inner]
        weights[first] = total * inverse[first]
    norm = weights[0]
    for pos in range(1, 5):
        norm = norm + weights[pos]
    scale = 1.0 / norm
    return [value * scale for value in weights]


OLD_PAIRS = [(first, second) for first in range(4) for second in range(first + 1)]


FAR_COL = sorted(
    [(over_y, over_x) for over_y in range(4) for over_x in range(4)][1:],
    key=lambda over: -sum(min(step, 4 - step) for step in over),
)
FAR_ROW = sorted(
    [(over_z, over_core) for over_z in range(8) for over_core in range(2)][1:],
    key=lambda over: -min(over[0], 8 - over[0]),
)


def lane_sums(left, right):
    return jnp.sum(left * right, axis=0, keepdims=True)


def main_kernel(
    iterate_ref, features_ref, input_weight_ref, mix_weight_ref, past_images_ref, past_residuals_ref, dense,
    state_out, residual_out,
    panel, acc, part, got1, sums, got2,
    state, inject, images, residuals, pack, gram_send1, gram_send2, gram_got1, gram_got2,
    load_sem, ag_send, ag_recv, rs1_send, rs1_recv, rs2_send, rs2_recv, gram_sem,
):
    row = lax.axis_index("row")
    col = lax.axis_index("col")
    z, core = row // 2, lax.rem(row, 2)
    y, x = col // 4, lax.rem(col, 4)
    first_axis, second_axis = (x, y), (y, x)
    sibling = row + 1 - 2 * core

    barrier = pltpu.get_barrier_semaphore()
    for (over_y, over_x), (over_z, over_core) in zip(FAR_COL, FAR_ROW):
        to_col = 4 * lax.rem(y + over_y, 4) + lax.rem(x + over_x, 4)
        to_row = 2 * lax.rem(z + over_z, 8) + lax.rem(core + over_core, 2)
        pl.semaphore_signal(barrier, inc=1, device_id=(row, to_col), device_id_type=MESH)
        pl.semaphore_signal(barrier, inc=1, device_id=(to_row, col), device_id_type=MESH)

    loads = []
    for half in range(2):
        for past_ref, kept in ((past_images_ref, images), (past_residuals_ref, residuals)):
            source = past_ref.at[pl.ds(1, 4), :, pl.ds(half * TILE, TILE)]
            loads.append(pltpu.make_async_copy(source, kept.at[pl.ds(0, 4), half], load_sem.at[len(loads)]))
            loads[-1].start()

    state[...] = iterate_ref[...]
    inject[...] = jnp.dot(features_ref[...], input_weight_ref[...], preferred_element_type=F32)
    pack[...] = jnp.zeros_like(pack)
    pl.semaphore_wait(barrier, 30)

    def chip(offset):
        return lax.rem(z + offset + 8, 8)

    def own_tile(offset):
        return 2 * chip(offset) + core

    def twin_tile(offset):
        return 2 * chip(offset) + 1 - core

    def gather_send(half, ref, target, slot, recv):
        return pltpu.make_async_remote_copy(
            src_ref=ref,
            dst_ref=ref,
            send_sem=ag_send.at[half, slot],
            recv_sem=ag_recv.at[half, recv],
            device_id=(target, col),
            device_id_type=MESH,
        )

    def gather_wait(half, tile, part=None, recv=None):
        ref = panel.at[half, tile] if part is None else panel.at[half, tile, part]
        pltpu.make_async_copy(ref, ref, ag_recv.at[half, tile if recv is None else recv]).wait()

    def multiply(halves, spots, first=False, last=False):
        tiles = [2 * spot + side for spot in spots for side in range(2)]
        rhs = jnp.concatenate(
            [jnp.concatenate([panel[half, tile] for tile in tiles], axis=0) for half in halves], axis=1
        )
        lhs = jnp.concatenate([dense[pl.ds(16 * tile, 16)].reshape(16 * TILE, TILE) for tile in tiles], axis=1)
        product = jnp.dot(lhs, rhs, preferred_element_type=F32)
        for pos, half in enumerate(halves):
            term = product[:, pos * TILE : (pos + 1) * TILE]
            if first:
                acc[half] = term
            elif not last:
                acc[half] += term
            else:
                total = (acc[half] + term).astype(BF16)
                for tile in range(16):
                    tile_y, tile_x = tile // 4, tile % 4
                    part[half, 0, tile_x, tile_y] = total[tile * TILE : tile * TILE + HALF]
                    part[half, 1, tile_y, tile_x] = total[tile * TILE + HALF : (tile + 1) * TILE]

    def all_waits(ref, sem):
        pltpu.make_async_copy(ref, ref, sem).wait()

    def scatter1(half, way, step):
        to = lax.rem(first_axis[way] + step, 4)
        return pltpu.make_async_remote_copy(
            src_ref=part.at[half, way, to], dst_ref=got1.at[half, way, first_axis[way]],
            send_sem=rs1_send.at[half, way], recv_sem=rs1_recv.at[half, way],
            device_id=(row, 4 * y + to if way == 0 else 4 * to + x), device_id_type=MESH,
        )

    def scatter2(half, way, step):
        to = lax.rem(second_axis[way] + step, 4)
        return pltpu.make_async_remote_copy(
            src_ref=sums.at[half, way, to], dst_ref=got2.at[half, way, second_axis[way]],
            send_sem=rs2_send.at[half, way], recv_sem=rs2_recv.at[half, way],
            device_id=(row, 4 * to + x if way == 0 else 4 * y + to), device_id_type=MESH,
        )

    def gram1(over_y, over_x):
        to = 4 * lax.rem(y + over_y, 4) + lax.rem(x + over_x, 4)
        return pltpu.make_async_remote_copy(
            src_ref=gram_send1, dst_ref=gram_got1.at[col], send_sem=gram_sem.at[0], recv_sem=gram_sem.at[1],
            device_id=(row, to), device_id_type=MESH,
        )

    def gram2(over_z, over_core):
        to = 2 * lax.rem(z + over_z, 8) + lax.rem(core + over_core, 2)
        return pltpu.make_async_remote_copy(
            src_ref=gram_send2, dst_ref=gram_got2.at[row], send_sem=gram_sem.at[2], recv_sem=gram_sem.at[3],
            device_id=(to, col), device_id_type=MESH,
        )

    @pl.loop(0, ITERS)
    def _(k):
        lowered = state[...].astype(BF16)
        sends = []
        used = [0, 0]

        def send(half, tile, target, part=None, recv=None):
            ref = panel.at[half, tile] if part is None else panel.at[half, tile, part]
            sends.append(gather_send(half, ref, target, used[half], tile if recv is None else recv))
            sends[-1].start()
            used[half] += 1

        for half in range(2):
            weight = mix_weight_ref[:, half * TILE : (half + 1) * TILE]
            panel[half, row] = jnp.dot(lowered, weight, preferred_element_type=F32).astype(BF16)
            for offset in (2, -2):
                send(half, row, own_tile(offset))
        for half in range(2):
            for offset in (1, -1, 0):
                send(half, row, sibling if offset == 0 else own_tile(offset))

        @pl.when(k > 0)
        def _():
            all_waits(gram_got1.at[pl.ds(0, 15)], gram_sem.at[0])
            all_waits(gram_got2.at[pl.ds(0, 15)], gram_sem.at[2])

        @pl.when(k == 0)
        def _():
            for load in loads:
                load.wait()

        for pos, (first, second) in enumerate(OLD_PAIRS):
            pack[5 + pos : 6 + pos, :] = sum(lane_sums(residuals[k + first, half], residuals[k + second, half]) for half in range(2))

        low, high = pl.ds(0, TILE // 2), pl.ds(TILE // 2, TILE // 2)

        def relay(half):
            for sign, part, extra in ((-1, low, None), (1, high, 16)):
                tile = own_tile(2 * sign)
                gather_wait(half, tile)
                send(half, tile, own_tile(-2 * sign), part, tile if extra is None else extra)
                send(half, tile, own_tile(-sign))
                send(half, tile, sibling)

        def adjacent(half):
            for sign in (-1, 1):
                gather_wait(half, own_tile(sign))
                send(half, own_tile(sign), sibling)

        def product(halves, *offsets, **where):
            for half in halves:
                for offset in offsets:
                    gather_wait(half, twin_tile(offset))
            multiply(halves, [chip(offset) for offset in offsets], **where)

        def distant(half):
            for offset in (-3, 3):
                gather_wait(half, own_tile(offset))
                send(half, own_tile(offset), sibling)
            gather_wait(half, own_tile(4), low)
            gather_wait(half, own_tile(4), high, 16)
            send(half, own_tile(4), sibling)

        def scatter(half):
            for step in (2, 1, 3):
                for way in range(2):
                    scatter1(half, way, step).start()

        relay(0)
        relay(1)
        adjacent(0)
        adjacent(1)
        product((0, 1), 0, first=True)
        product((0, 1), 1, -1)
        distant(0)
        distant(1)
        product((0, 1), 2, -2)
        product((0,), 3, -3)
        product((0,), 4, last=True)
        scatter(0)
        product((1,), 3, -3)
        product((1,), 4, last=True)
        scatter(1)

        for half in range(2):
            for way in range(2):
                all_waits(got1.at[half, way, pl.ds(0, 3)], rs1_recv.at[half, way])
                total = part[half, way, first_axis[way]].astype(F32)
                for step in range(1, 4):
                    total += got1[half, way, lax.rem(first_axis[way] + step, 4)].astype(F32)
                sums[half, way] = total.astype(BF16)
                for step in (2, 1, 3):
                    scatter2(half, way, step).start()

        scores = [0.0] * 5
        for half in range(2):
            lanes = slice(half * TILE, (half + 1) * TILE)
            for way in range(2):
                rows = slice(way * HALF, (way + 1) * HALF)
                all_waits(got2.at[half, way, pl.ds(0, 3)], rs2_recv.at[half, way])
                total = sums[half, way, second_axis[way]].astype(F32)
                for step in range(1, 4):
                    total += got2[half, way, lax.rem(second_axis[way] + step, 4)].astype(F32)
                image = jnp.maximum(total + inject[rows, lanes], 0.0)
                residual = image - state[rows, lanes]
                images[k + 4, half, rows] = image
                residuals[k + 4, half, rows] = residual
                for pos in range(5):
                    other = residual if pos == 4 else residuals[k + pos, half, rows]
                    scores[pos] = scores[pos] + lane_sums(residual, other)

        for pos in range(5):
            pack[pos : pos + 1, :] = scores[pos]
        head, tail = pack[0:8], pack[8:16]
        lanes = lax.broadcasted_iota(jnp.int32, (8, TILE), 1)
        own = jnp.where(lanes < 64, head + pltpu.roll(head, 64, 1), tail + pltpu.roll(tail, 64, 1))
        gram_send1[...] = own
        gram_got1[col] = own

        for over in FAR_COL:
            gram1(*over).start()

        for copy in sends:
            copy.wait_send()

        for half in range(2):
            for way in range(2):
                all_waits(part.at[half, way, pl.ds(0, 3)], rs1_send.at[half, way])
                all_waits(sums.at[half, way, pl.ds(0, 3)], rs2_send.at[half, way])
        all_waits(gram_got1.at[pl.ds(0, 15)], gram_sem.at[1])

        own = jnp.sum(gram_got1[...], axis=0)
        gram_send2[...] = own
        gram_got2[row] = own

        for over in FAR_ROW:
            gram2(*over).start()

        all_waits(gram_got2.at[pl.ds(0, 15)], gram_sem.at[3])

        whole = jnp.sum(gram_got2[...], axis=0)
        head = jnp.sum(jnp.where(lanes < 64, whole, 0.0), axis=1, keepdims=True)
        tail = jnp.sum(jnp.where(lanes < 64, 0.0, whole), axis=1, keepdims=True)
        head = jnp.broadcast_to(head, (8, TILE))
        tail = jnp.broadcast_to(tail, (8, TILE))
        values = [head[pos : pos + 1] for pos in range(8)] + [tail[pos : pos + 1] for pos in range(8)]
        gram = {(4, pos): values[pos] for pos in range(5)}
        for pos, pair in enumerate(OLD_PAIRS):
            gram[pair] = values[5 + pos]
        alpha = mixing_weights(gram)
        for half in range(2):
            mixed = alpha[0] * images[k, half]
            for pos in range(1, 5):
                mixed += alpha[pos] * images[k + pos, half]
            state[:, half * TILE : (half + 1) * TILE] = mixed

    all_waits(gram_got1.at[pl.ds(0, 15)], gram_sem.at[0])
    all_waits(gram_got2.at[pl.ds(0, 15)], gram_sem.at[2])
    state_out[...] = state[...]
    for half in range(2):
        residual_out[:, half * TILE : (half + 1) * TILE] = residuals[ITERS + 3, half]


def on_device(
    iterate,
    past_images,
    past_residuals,
    features,
    input_weight,
    mix_weight,
    tile_values,
    tile_rows,
    tile_cols,
    tile_count,
):
    dense = build_dense((tile_cols * 16 + tile_rows)[0, 0], tile_count[0], tile_values[0, 0])
    dma = pltpu.SemaphoreType.DMA
    vmem = pl.BlockSpec(memory_space=pltpu.VMEM)
    hbm = pl.BlockSpec(memory_space=pl.ANY)
    block = jax.ShapeDtypeStruct((TILE, CHANNELS), F32)
    history = pltpu.VMEM((ITERS + 4, 2, TILE, TILE), F32)
    quads = pltpu.VMEM((2, 2, 4, 4, HALF, TILE), BF16)
    singles = pltpu.VMEM((2, 2, 4, HALF, TILE), BF16)
    return pl.pallas_call(
        main_kernel,
        out_shape=(block, block),
        in_specs=[vmem] * 4 + [hbm] * 2 + [vmem],
        out_specs=(vmem, vmem),
        scratch_shapes=[
            pltpu.VMEM((2, 16, TILE, TILE), BF16),
            pltpu.VMEM((2, 16 * TILE, TILE), F32),
            quads, quads, singles, singles,
            pltpu.VMEM((TILE, CHANNELS), F32),
            pltpu.VMEM((TILE, CHANNELS), F32),
            history,
            history,
            pltpu.VMEM((16, TILE), F32),
            pltpu.VMEM((8, TILE), F32),
            pltpu.VMEM((8, TILE), F32),
            pltpu.VMEM((16, 8, TILE), F32),
            pltpu.VMEM((16, 8, TILE), F32),
            dma((4,)), dma((2, 16)), dma((2, 17)), dma((2, 2)), dma((2, 2)), dma((2, 2)), dma((2, 2)), dma((4,)),
        ],
        compiler_params=pltpu.CompilerParams(
            collective_id=0, has_side_effects=True, vmem_limit_bytes=24 * 1024 * 1024
        ),
        name="anderson",
    )(iterate, features, input_weight, mix_weight, past_images, past_residuals, dense)


def solution(mesh):
    return jax.shard_map(
        on_device,
        mesh=mesh,
        in_specs=(
            P(("row", "col"), None),
            P(None, ("row", "col"), None),
            P(None, ("row", "col"), None),
            P(("row", "col"), None),
            P(),
            P(),
            P("row", "col", None, None, None),
            P("row", "col", None),
            P("row", "col", None),
            P("row", "col"),
        ),
        out_specs=(P(("row", "col"), None), P(("row", "col"), None)),
        check_vma=False,
    )
```
